128 devices in a mesh: tok: 16 (over y, z), voc: 8 (over x, core).
Axes of the slice: x: 4, y: 4, z: 4, core: 2. Of those that a mesh axis runs over, the one named last changes fastest.
Arguments:
- hidden: bfloat16 [2048, 3584], P('tok', 'voc'), may hold values from -36 to 36
- weight: bfloat16 [3584, 256000], P(None, ('voc', 'tok')), may hold values from -1 to 1
- targets: int32 [2048], replicated, may hold values from 0 to 255999
- slot: int32 [16], replicated, may hold values from 0 to 15, each once
- prompt_len: int32 [16], replicated, may hold values from 1 to 64
- ref_means: float32 [16], replicated, may hold values from -17 to -13
Outputs:
- token_logprobs: float32 [2048], P('tok')
- margins: float32 [8], replicated
- loss: float32 [], replicated
The draws below stay inside these ranges and needn't reach their ends.
All inputs are finite; a program needn't handle non-finite values.
Results may differ from the reference program's by a relative error of at most 0.0003.
Values may be sent and summed in bfloat16 or wider, within the bound.
No kernel may reach another device: no remote copies, remote signals or barrier semaphores. Data moves between devices by JAX's collectives and lax.ppermute only.
A program may use at most 128 MiB of HBM per device.

```python
import math
import jax
import jax.numpy as jnp
import numpy as np
from jax import lax

D = 3584
V = 256000
SEQLEN = 128
TOKENS = 2048
SEQS = 16


def weight_block(key, blk_id):
    weight_key = jax.random.fold_in(key, 11)
    return jnp.clip(jax.random.normal(jax.random.fold_in(weight_key, blk_id), (D, 128), jnp.float32), -5.0, 5.0)


def draw_weight(key, part):
    blocks = jax.vmap(lambda blk_id: weight_block(key, blk_id))(jnp.arange(V // 128, dtype=jnp.int32))
    whole = jnp.transpose(blocks, (1, 0, 2)).reshape(D, V)
    whole = jnp.clip(whole / math.sqrt(D), -1.0, 1.0)
    return whole.astype(jnp.bfloat16)


def draw_hidden(key, part):
    base = jnp.clip(jax.random.normal(jax.random.fold_in(key, 21), (TOKENS, D), jnp.float32), -5.0, 5.0)
    values = 3.0 * base
    return values.astype(jnp.bfloat16)


def place_ends(result, own_key, least, top_value):
    shape = result.shape
    index_at = [jax.random.randint(jax.random.fold_in(own_key, axis), (), 0, shape[axis]) for axis in range(len(shape))]
    result = result.at[tuple(index_at)].set(least)
    longest = shape.index(max(shape))
    index_at[longest] = (index_at[longest] + 1) % shape[longest]
    return result.at[tuple(index_at)].set(top_value)


def skewed_wide(rng, dims, number_of, skew):
    weights = [min(1 << octave, number_of + 1 - (1 << octave)) * (1 << 20) // math.isqrt((1 << octave) ** skew) + 1 for octave in range((number_of + 1).bit_length()) if 1 << octave <= number_of]
    deviation = 1 + sum(weights) // (1 << 30)
    grid = np.cumsum(np.array([max(1, weight // deviation) for weight in weights]))
    lot = jax.random.randint(jax.random.fold_in(rng, 1), dims, 0, int(grid[len(weights) - 1]))
    start = jnp.left_shift(1, jnp.searchsorted(jnp.asarray(grid, jnp.int32), lot, side="right").astype(jnp.int32))
    rank = start - 1 + jax.random.randint(jax.random.fold_in(rng, 4), dims, 0, 1 << 30) % jnp.minimum(start, number_of + 1 - start)
    return jax.random.permutation(jax.random.fold_in(rng, 2), number_of)[rank].astype(jnp.int32)


def setup_inputs(seed: int = 0) -> dict:
    key_list = jax.random.split(jax.random.key(seed), 7)
    return {
        "hidden": draw_hidden(jax.random.fold_in(key_list[6], 71), 0),
        "weight": draw_weight(jax.random.fold_in(key_list[6], 71), 0),
        "targets": place_ends(skewed_wide(key_list[2], (TOKENS,), V, 2), jax.random.fold_in(key_list[2], 3), 0, V - 1).astype(jnp.int32),
        "slot": jax.random.permutation(key_list[3], SEQS).astype(jnp.int32),
        "prompt_len": place_ends(jax.random.randint(key_list[4], (SEQS,), 1, SEQLEN // 2 + 1), jax.random.fold_in(key_list[4], 1), 1, (SEQLEN // 2 + 1) - 1).astype(jnp.int32),
        "ref_means": jnp.clip(jax.random.uniform(key_list[5], (SEQS,), jnp.float32, -17.0, -13.0), -17.0, -13.0),
    }


beta_scale = 2.0


def finish(token_lp, slot, prompt_len, ref_means):
    seq_count = slot.shape[0]
    per_seq = token_lp.reshape(seq_count, -1)
    seq_width = per_seq.shape[1]
    position = jnp.arange(seq_width, dtype=jnp.int32)[None, :]
    in_reply = position >= prompt_len[:, None]
    reply_len = (seq_width - prompt_len).astype(jnp.float32)
    seq_means = jnp.sum(jnp.where(in_reply, per_seq, jnp.float32(0.0)), axis=1) / reply_len
    advantage = seq_means - ref_means
    polarity = jnp.where(slot % 2 == 0, jnp.float32(1.0), jnp.float32(-1.0))
    n_pairs = seq_count // 2
    onehot = (slot[:, None] // 2) == jnp.arange(n_pairs, dtype=jnp.int32)[None, :]
    signed = (polarity * advantage)[:, None]
    margins = beta_scale * jnp.sum(jnp.where(onehot, signed, jnp.float32(0.0)), axis=0)
    pair_loss = jnp.mean(jax.nn.softplus(-margins))
    return margins, pair_loss


def reference(hidden, weight, targets, slot, prompt_len, ref_means):
    blocks = hidden.reshape(TOKENS // SEQLEN, SEQLEN, D)
    target_blocks = targets.reshape(TOKENS // SEQLEN, SEQLEN)

    def one_block(operands):
        rows_h, rows_t = operands
        logits = jnp.dot(rows_h, weight, preferred_element_type=jnp.float32)
        row_max = jnp.max(logits, axis=1)
        row_sum = jnp.sum(jnp.exp(logits - row_max[:, None]), axis=1)
        picked = jnp.take_along_axis(logits, rows_t[:, None].astype(jnp.int32), axis=1)[:, 0]
        return picked - (row_max + jnp.log(row_sum))

    token_lp = lax.map(one_block, (blocks, target_blocks)).reshape(TOKENS)
    margins, pair_loss = finish(token_lp, slot, prompt_len, ref_means)
    return token_lp, margins, pair_loss
```

```python
import functools

import jax
import jax.numpy as jnp
from jax import lax
from jax.experimental import pallas as pl
from jax.experimental.pallas import tpu as pltpu
from jax.sharding import Mesh
from jax.sharding import PartitionSpec as P

Y, Z, X, C = "tok_0", "tok_1", "voc_0", "voc_1"
VOC = (X, C)
TOK = (Y, Z)
VOC_TOK = (X, C, Y, Z)
CHIPS = (Y, Z, X)
EVERY = (Y, Z, X, C)

RING = 4
SWAP = [(0, 1), (1, 0)]
PLACE = (0, 2, 3, 1)
BLOCK_ROWS = 400

beta_scale = 2.0


def ring_pairs(step):
    return [(i, (i + step) % RING) for i in range(RING)]


def crossed_pairs(first, step):
    pairs = []
    for y in range(4):
        for z in range(4):
            for x in range(4):
                for c in range(2):
                    along_z = (c == 0) == first
                    y2, z2 = (y, (z + step) % RING) if along_z else ((y + step) % RING, z)
                    pairs.append((((y * 4 + z) * 4 + x) * 2 + c, ((y2 * 4 + z2) * 4 + x) * 2 + c))
    return pairs


def shifted(block, first, step):
    return lax.ppermute(block, EVERY, crossed_pairs(first, step))


def finish(per_seq, slot, prompt_len, ref_means):
    seq_count, seq_width = per_seq.shape
    position = jnp.arange(seq_width, dtype=jnp.int32)[None, :]
    in_reply = position >= prompt_len[:, None]
    reply_len = (seq_width - prompt_len).astype(jnp.float32)
    seq_means = jnp.sum(jnp.where(in_reply, per_seq, jnp.float32(0.0)), axis=1) / reply_len
    advantage = seq_means - ref_means
    polarity = jnp.where(slot % 2 == 0, jnp.float32(1.0), jnp.float32(-1.0))
    n_pairs = seq_count // 2
    onehot = slot[:, None] // 2 == jnp.arange(n_pairs, dtype=jnp.int32)[None, :]
    signed = (polarity * advantage)[:, None]
    margins = beta_scale * jnp.sum(jnp.where(onehot, signed, jnp.float32(0.0)), axis=0)
    pair_loss = jnp.mean(jax.nn.softplus(-margins))
    return (margins, pair_loss)


def stats_kernel(local_ids, *refs, counts):
    n_in = len(counts)
    parts = refs[:n_in]
    w_own, w_other, out, rows, top, total, picked = refs[n_in:]
    width = rows.shape[1]
    step = pl.program_id(0)

    @pl.when(step == 0)
    def _():
        pieces = [(ref, k) for ref, n in zip(parts, counts) for k in range(n)]
        for p in range(len(pieces) // 2):
            (ref_a, ka), (ref_b, kb) = pieces[2 * p], pieces[2 * p + 1]
            lanes = slice(p * 128, (p + 1) * 128)
            for x in range(4):
                a = ref_a[ka * 1792 + x * 448 : ka * 1792 + (x + 1) * 448, :]
                b = ref_b[kb * 1792 + x * 448 : kb * 1792 + (x + 1) * 448, :]
                rows[2 * x * 448 : (2 * x + 1) * 448, lanes] = jnp.concatenate([a[:, :64], b[:, :64]], 1)
                rows[(2 * x + 1) * 448 : (2 * x + 2) * 448, lanes] = jnp.concatenate([a[:, 64:], b[:, 64:]], 1)
        top[...] = jnp.full_like(top, -jnp.inf)
        total[...] = jnp.zeros_like(total)
        picked[...] = jnp.zeros_like(picked)

    for k, w in enumerate((w_own, w_other)):
        logits = jnp.dot(w[...], rows[...], preferred_element_type=jnp.float32)
        tiles = logits.reshape(BLOCK_ROWS // 8, 8, width)
        before = top[...]
        now = jnp.maximum(before, jnp.max(tiles, 0))
        total[...] = total[...] * jnp.exp(before - now) + jnp.sum(jnp.exp(tiles - now[None]), 0)
        top[...] = now
        ids = lax.broadcasted_iota(jnp.int32, (BLOCK_ROWS, width), 0)
        hit = ids == local_ids[k : k + 1, :] - step * BLOCK_ROWS
        picked[...] += jnp.sum(jnp.where(hit, logits, 0.0).reshape(BLOCK_ROWS // 8, 8, width), 0)

    @pl.when(step == pl.num_programs(0) - 1)
    def _():
        peak = jnp.max(top[...], 0, keepdims=True)
        mass = jnp.sum(total[...] * jnp.exp(top[...] - peak), 0, keepdims=True)
        out[0:1, :] = peak + jnp.log(mass)
        out[1:2, :] = jnp.sum(picked[...], 0, keepdims=True)


def chunk_stats(w_own, w_other, local_ids, *parts):
    counts = tuple(part.shape[0] // 1792 for part in parts)
    width = 64 * sum(counts)
    vocab, depth = w_own.shape
    whole = lambda shape: pl.BlockSpec(shape, lambda i: (0, 0))
    once = lambda shape: pl.BlockSpec(shape, lambda i: (0, 0), pipeline_mode=pl.Buffered(1))
    tile = pl.BlockSpec((BLOCK_ROWS, depth), lambda i: (i, 0))
    return pl.pallas_call(
        functools.partial(stats_kernel, counts=counts),
        grid=(vocab // BLOCK_ROWS,),
        in_specs=[whole((2, width))] + [once(part.shape) for part in parts] + [tile, tile],
        out_specs=whole((2, width)),
        out_shape=jax.ShapeDtypeStruct((2, width), jnp.float32),
        scratch_shapes=[pltpu.VMEM((depth, width), jnp.bfloat16)] + [pltpu.VMEM((8, width), jnp.float32)] * 3,
        compiler_params=pltpu.CompilerParams(vmem_limit_bytes=40 * 2**20),
        cost_estimate=pl.CostEstimate(
            flops=4 * width * vocab * depth, bytes_accessed=4 * vocab * depth, transcendentals=2 * vocab * width
        ),
    )(local_ids, *parts, pltpu.with_memory_space_constraint(w_own, pltpu.HBM), pltpu.with_memory_space_constraint(w_other, pltpu.HBM))


def body(hidden, weight, targets, slot, prompt_len, ref_means):
    y, z, x, c = (lax.axis_index(axis) for axis in EVERY)
    vocab_cols = weight.shape[1]
    w_own = weight.T
    mine = hidden.T

    theirs = lax.ppermute(mine, C, SWAP)
    low = jnp.concatenate([mine[:, :64], theirs[:, :64]], 1)
    high = jnp.concatenate([theirs[:, 64:], mine[:, 64:]], 1)
    half = jnp.where(c == 0, low, high)
    behind, ahead, across = (lax.ppermute(half, X, ring_pairs(s)) for s in (1, 3, 2))
    turned = jnp.concatenate([half, ahead, across, behind, half, ahead, across], 0)
    own = lax.dynamic_slice_in_dim(turned, lax.rem(4 - x, 4) * 448, 1792, 0)

    w_other = lax.ppermute(w_own, C, SWAP)

    group = jnp.arange(16, dtype=jnp.int32)
    offset = jnp.array([0, 3, 1, 2], jnp.int32)
    off_a, off_b = offset[group % 4], offset[group // 4]
    off_y, off_z = jnp.where(c == 0, off_b, off_a), jnp.where(c == 0, off_a, off_b)
    source = (y + off_y) % 4 * 4 + (z + off_z) % 4
    ids = jnp.take(targets.reshape(32, 64), source * 2 + c, axis=0).reshape(1, 1024)
    start = lambda core: (((x * 2 + core) * 4 + y) * 4 + z) * vocab_cols
    local_ids = jnp.concatenate([ids - start(c), ids - start(1 - c)], 0)

    a_behind, a_ahead = shifted(own, True, 1), shifted(own, True, 3)
    a_across = [shifted(a_behind[:896], True, 1), shifted(a_ahead[896:], True, 3)]
    chunk = jnp.concatenate([own, a_behind, a_ahead, *a_across], 0)
    b_behind, b_ahead = shifted(chunk, False, 1), shifted(chunk, False, 3)
    first = chunk_stats(w_own, w_other, local_ids[:, :256], chunk)
    b_behind, b_ahead, first = lax.optimization_barrier((b_behind, b_ahead, first))
    b_across = [shifted(b_behind[:3584], False, 1), shifted(b_ahead[3584:], False, 3)]

    second = chunk_stats(w_own, w_other, local_ids[:, 256:768], b_behind, b_ahead)
    b_across = lax.optimization_barrier((b_across, second))
    b_across, second = b_across
    third = chunk_stats(w_own, w_other, local_ids[:, 768:], *b_across)
    stats = jnp.concatenate([first, second, third], 1).reshape(2, 16, 64)

    group_y, group_z = (group // 4 - y) % 4, (group % 4 - z) % 4
    place = jnp.array(PLACE, jnp.int32)
    at_a, at_b = place[jnp.where(c == 0, group_z, group_y)], place[jnp.where(c == 0, group_y, group_z)]
    stats = jnp.take(stats, at_b * 4 + at_a, axis=1).reshape(2, 1024)

    copies = jnp.broadcast_to(stats, (64, 2, 1024))
    parts = lax.all_to_all(copies, CHIPS, split_axis=0, concat_axis=0, tiled=True)
    peak = jnp.max(parts[:, 0], 0)
    mass = jnp.sum(jnp.exp(parts[:, 0] - peak), 0)
    token_lp = (jnp.sum(parts[:, 1], 0) - (peak + jnp.log(mass))).reshape(16, 64)
    other_lp = lax.ppermute(token_lp, C, SWAP)
    per_seq = jnp.where(
        c == 0, jnp.concatenate([token_lp, other_lp], 1), jnp.concatenate([other_lp, token_lp], 1)
    )
    own_rows = lax.dynamic_slice_in_dim(per_seq, y * 4 + z, 1, 0).reshape(128)
    margins, pair_loss = finish(per_seq, slot, prompt_len, ref_means)
    return (own_rows, margins, pair_loss)


def solution(mesh):
    split = Mesh(mesh.devices.reshape(4, 4, 4, 2), EVERY)
    in_specs = (P(TOK, VOC), P(None, VOC_TOK), P(), P(), P(), P())
    out_specs = (P(TOK), P(), P())
    return jax.shard_map(body, mesh=split, in_specs=in_specs, out_specs=out_specs, check_vma=False)
```

```python
import functools

import jax
import jax.numpy as jnp
import numpy as np
from jax import lax
from jax.experimental import pallas as pl
from jax.experimental.pallas import tpu as pltpu
from jax.sharding import Mesh
from jax.sharding import PartitionSpec as P

Y, Z, X, C = "tok_0", "tok_1", "voc_0", "voc_1"
VOC = (X, C)
TOK = (Y, Z)
VOC_TOK = (X, C, Y, Z)
CHIPS = (Y, Z, X)
EVERY = (Y, Z, X, C)

RING = 4
SWAP = [(0, 1), (1, 0)]
ALONG_A = np.array([0, 3, 1, 2, 0, 3, 1, 2, 1, 2, 0, 3, 0, 3, 1, 2], np.int32)
ALONG_B = np.array([0, 0, 0, 0, 3, 3, 1, 1, 3, 3, 1, 1, 2, 2, 2, 2], np.int32)
PLACE = np.zeros(16, np.int32)
PLACE[ALONG_A * 4 + ALONG_B] = np.arange(16)
ROWS = 1792
BLOCK_ROWS = 400
AHEAD = 3

beta_scale = 2.0


def ring_pairs(step):
    return [(i, (i + step) % RING) for i in range(RING)]


def crossed_pairs(first, step):
    pairs = []
    for y in range(4):
        for z in range(4):
            for x in range(4):
                for c in range(2):
                    along_z = (c == 0) == first
                    y2, z2 = (y, (z + step) % RING) if along_z else ((y + step) % RING, z)
                    pairs.append((((y * 4 + z) * 4 + x) * 2 + c, ((y2 * 4 + z2) * 4 + x) * 2 + c))
    return pairs


def shifted(block, first, step):
    return lax.ppermute(block, EVERY, crossed_pairs(first, step))


def finish(per_seq, slot, prompt_len, ref_means):
    seq_count, seq_width = per_seq.shape
    position = jnp.arange(seq_width, dtype=jnp.int32)[None, :]
    in_reply = position >= prompt_len[:, None]
    reply_len = (seq_width - prompt_len).astype(jnp.float32)
    seq_means = jnp.sum(jnp.where(in_reply, per_seq, jnp.float32(0.0)), axis=1) / reply_len
    advantage = seq_means - ref_means
    polarity = jnp.where(slot % 2 == 0, jnp.float32(1.0), jnp.float32(-1.0))
    n_pairs = seq_count // 2
    onehot = slot[:, None] // 2 == jnp.arange(n_pairs, dtype=jnp.int32)[None, :]
    signed = (polarity * advantage)[:, None]
    margins = beta_scale * jnp.sum(jnp.where(onehot, signed, jnp.float32(0.0)), axis=0)
    pair_loss = jnp.mean(jax.nn.softplus(-margins))
    return (margins, pair_loss)


def stats_kernel(local_ids, *refs, counts):
    n_in = len(counts)
    parts = refs[:n_in]
    *far, out, near, rows, top, total, picked, arrived = refs[n_in:]
    width = rows.shape[1]
    steps = near.shape[1] // BLOCK_ROWS

    def block(i):
        return pl.ds(pl.multiple_of(i * BLOCK_ROWS, BLOCK_ROWS), BLOCK_ROWS)

    def bringing(k, i):
        return pltpu.make_async_copy(far[k].at[block(i), :], near.at[k, block(i), :], arrived.at[k, i])

    for i in range(AHEAD):
        bringing(0, i).start()

    pieces = [(ref, k * ROWS) for ref, n in zip(parts, counts) for k in range(n)]
    for p in range(len(pieces) // 2):
        (ref_a, at_a), (ref_b, at_b) = pieces[2 * p], pieces[2 * p + 1]
        lanes = slice(p * 128, (p + 1) * 128)
        for x in range(4):
            a = ref_a[at_a + x * 448 : at_a + (x + 1) * 448, :]
            b = ref_b[at_b + x * 448 : at_b + (x + 1) * 448, :]
            rows[2 * x * 448 : (2 * x + 1) * 448, lanes] = jnp.concatenate([a[:, :64], b[:, :64]], 1)
            rows[(2 * x + 1) * 448 : (2 * x + 2) * 448, lanes] = jnp.concatenate([a[:, 64:], b[:, 64:]], 1)
    top[...] = jnp.full_like(top, -jnp.inf)
    total[...] = jnp.zeros_like(total)
    picked[...] = jnp.zeros_like(picked)

    for k in range(2):

        def step(i, carry):
            later = i + AHEAD

            @pl.when(later < steps)
            def _():
                bringing(k, later).start()

            if k == 0:

                @pl.when(later >= steps)
                def _():
                    bringing(1, later - steps).start()

            bringing(k, i).wait()
            logits = jnp.dot(near[k, block(i), :], rows[...], preferred_element_type=jnp.float32)
            tiles = logits.reshape(BLOCK_ROWS // 8, 8, width)
            before = top[...]
            now = jnp.maximum(before, jnp.max(tiles, 0))
            total[...] = total[...] * jnp.exp(before - now) + jnp.sum(jnp.exp(tiles - now[None]), 0)
            top[...] = now
            ids = lax.broadcasted_iota(jnp.int32, (BLOCK_ROWS, width), 0)
            hit = ids == local_ids[k : k + 1, :] - i * BLOCK_ROWS
            picked[...] += jnp.sum(jnp.where(hit, logits, 0.0).reshape(BLOCK_ROWS // 8, 8, width), 0)
            return carry

        lax.fori_loop(0, steps, step, 0)
    peak = jnp.max(top[...], 0, keepdims=True)
    mass = jnp.sum(total[...] * jnp.exp(top[...] - peak), 0, keepdims=True)
    out[0:1, :] = peak + jnp.log(mass)
    out[1:2, :] = jnp.sum(picked[...], 0, keepdims=True)


def chunk_stats(weights, local_ids, *parts):
    counts = tuple(part.shape[0] // ROWS for part in parts)
    width = 64 * sum(counts)
    vocab, depth = weights[0].shape
    near = pl.BlockSpec(memory_space=pltpu.VMEM)
    held = lambda arrays: [pltpu.with_memory_space_constraint(array, pltpu.VMEM) for array in arrays]
    far = pl.BlockSpec(memory_space=pl.ANY)
    return pl.pallas_call(
        functools.partial(stats_kernel, counts=counts),
        in_specs=[near] * (1 + len(parts)) + [far, far],
        out_specs=near,
        out_shape=jax.ShapeDtypeStruct((2, width), jnp.float32),
        scratch_shapes=[pltpu.VMEM((2, vocab, depth), jnp.bfloat16), pltpu.VMEM((depth, width), jnp.bfloat16)]
        + [pltpu.VMEM((8, width), jnp.float32)] * 3
        + [pltpu.SemaphoreType.DMA((2, vocab // BLOCK_ROWS))],
        compiler_params=pltpu.CompilerParams(vmem_limit_bytes=(width // 256 * 8 + 31) * 2**20),
        cost_estimate=pl.CostEstimate(
            flops=4 * width * vocab * depth, bytes_accessed=4 * vocab * depth, transcendentals=2 * vocab * width
        ),
    )(local_ids, *held(parts), *[pltpu.with_memory_space_constraint(w, pltpu.HBM) for w in weights])


def body(hidden, weight, targets, slot, prompt_len, ref_means):
    y, z, x, c = (lax.axis_index(axis) for axis in EVERY)
    vocab_cols = weight.shape[1]
    w_own = weight.T
    mine = hidden.T

    theirs = lax.ppermute(mine, C, SWAP)
    theirs, weight_sent = lax.optimization_barrier((theirs, w_own))
    w_other = lax.ppermute(weight_sent, C, SWAP)
    weights = [w_own, w_other]
    low = jnp.concatenate([mine[:, :64], theirs[:, :64]], 1)
    high = jnp.concatenate([theirs[:, 64:], mine[:, 64:]], 1)
    half = jnp.where(c == 0, low, high)
    behind, ahead, across = (lax.ppermute(half, X, ring_pairs(s)) for s in (1, 3, 2))
    turned = jnp.concatenate([half, ahead, across, behind, half, ahead, across], 0)
    own = lax.dynamic_slice_in_dim(turned, lax.rem(4 - x, 4) * 448, 1792, 0)

    off_y, off_z = jnp.where(c == 0, ALONG_B, ALONG_A), jnp.where(c == 0, ALONG_A, ALONG_B)
    source = (y + off_y) % 4 * 4 + (z + off_z) % 4
    ids = jnp.take(targets.reshape(32, 64), source * 2 + c, axis=0).reshape(1, 1024)
    start = lambda core: (((x * 2 + core) * 4 + y) * 4 + z) * vocab_cols
    local_ids = jnp.concatenate([ids - start(c), ids - start(1 - c)], 0)

    a_behind, a_ahead, *a_across = (shifted(own, True, k) for k in (1, 3, 2))
    upper = jnp.concatenate([own, a_behind], 0)
    lower = jnp.concatenate([a_ahead, *a_across], 0)
    behind_upper, ahead_lower = shifted(upper, False, 1), shifted(lower, False, 3)
    behind_lower, ahead_upper = shifted(lower, False, 1), shifted(upper, False, 3)
    first = chunk_stats(weights, local_ids[:, :256], upper, lower)
    behind_upper, ahead_lower, first = lax.optimization_barrier((behind_upper, ahead_lower, first))
    across = [shifted(behind_upper, False, 1), shifted(ahead_lower, False, 3)]
    second = chunk_stats(weights, local_ids[:, 256:512], behind_upper, ahead_lower)
    behind_lower, ahead_upper, across, second = lax.optimization_barrier((behind_lower, ahead_upper, across, second))
    third = chunk_stats(weights, local_ids[:, 512:], behind_lower, ahead_upper, *across)
    stats = jnp.concatenate([first, second, third], 1).reshape(2, 16, 64)
    group = np.arange(16, dtype=np.int32)
    ahead_y, ahead_z = (group // 4 - y) % 4, (group % 4 - z) % 4
    at = jnp.take(PLACE, jnp.where(c == 0, ahead_z * 4 + ahead_y, ahead_y * 4 + ahead_z), axis=0)
    stats = jnp.take(stats, at, axis=1).reshape(2, 1024)

    copies = jnp.broadcast_to(stats, (64, 2, 1024))
    parts = lax.all_to_all(copies, CHIPS, split_axis=0, concat_axis=0, tiled=True)
    peak = jnp.max(parts[:, 0], 0)
    mass = jnp.sum(jnp.exp(parts[:, 0] - peak), 0)
    token_lp = (jnp.sum(parts[:, 1], 0) - (peak + jnp.log(mass))).reshape(16, 64)
    other_lp = lax.ppermute(token_lp, C, SWAP)
    per_seq = jnp.where(
        c == 0, jnp.concatenate([token_lp, other_lp], 1), jnp.concatenate([other_lp, token_lp], 1)
    )
    own_rows = lax.dynamic_slice_in_dim(per_seq, y * 4 + z, 1, 0).reshape(128)
    margins, pair_loss = finish(per_seq, slot, prompt_len, ref_means)
    return (own_rows, margins, pair_loss)


def solution(mesh):
    split = Mesh(mesh.devices.reshape(4, 4, 4, 2), EVERY)
    in_specs = (P(TOK, VOC), P(None, VOC_TOK), P(), P(), P(), P())
    out_specs = (P(TOK), P(), P())
    return jax.shard_map(body, mesh=split, in_specs=in_specs, out_specs=out_specs, check_vma=False)
```

```python
import functools

import jax
import jax.numpy as jnp
import numpy as np
from jax import lax
from jax.experimental import pallas as pl
from jax.experimental.pallas import tpu as pltpu
from jax.sharding import Mesh
from jax.sharding import PartitionSpec as P

Y, Z, X, C = "tok_0", "tok_1", "voc_0", "voc_1"
VOC = (X, C)
TOK = (Y, Z)
VOC_TOK = (X, C, Y, Z)
CHIPS = (Y, Z, X)
EVERY = (Y, Z, X, C)

RING = 4
SWAP = [(0, 1), (1, 0)]
ALONG_A = np.array([0, 3, 1, 2, 0, 3, 1, 2, 1, 2, 0, 3, 0, 3, 1, 2], np.int32)
ALONG_B = np.array([0, 0, 0, 0, 3, 3, 1, 1, 3, 3, 1, 1, 2, 2, 2, 2], np.int32)
PLACE = np.zeros(16, np.int32)
PLACE[ALONG_A * 4 + ALONG_B] = np.arange(16)
ROWS = 1792
BLOCK_ROWS = 400
AHEAD = 2

beta_scale = 2.0


def ring_pairs(step):
    return [(i, (i + step) % RING) for i in range(RING)]


def crossed_pairs(first, step):
    pairs = []
    for y in range(4):
        for z in range(4):
            for x in range(4):
                for c in range(2):
                    along_z = (c == 0) == first
                    y2, z2 = (y, (z + step) % RING) if along_z else ((y + step) % RING, z)
                    pairs.append((((y * 4 + z) * 4 + x) * 2 + c, ((y2 * 4 + z2) * 4 + x) * 2 + c))
    return pairs


def shifted(block, first, step):
    return lax.ppermute(block, EVERY, crossed_pairs(first, step))


def finish(per_seq, slot, prompt_len, ref_means):
    seq_count, seq_width = per_seq.shape
    position = jnp.arange(seq_width, dtype=jnp.int32)[None, :]
    in_reply = position >= prompt_len[:, None]
    reply_len = (seq_width - prompt_len).astype(jnp.float32)
    seq_means = jnp.sum(jnp.where(in_reply, per_seq, jnp.float32(0.0)), axis=1) / reply_len
    advantage = seq_means - ref_means
    polarity = jnp.where(slot % 2 == 0, jnp.float32(1.0), jnp.float32(-1.0))
    n_pairs = seq_count // 2
    onehot = slot[:, None] // 2 == jnp.arange(n_pairs, dtype=jnp.int32)[None, :]
    signed = (polarity * advantage)[:, None]
    margins = beta_scale * jnp.sum(jnp.where(onehot, signed, jnp.float32(0.0)), axis=0)
    pair_loss = jnp.mean(jax.nn.softplus(-margins))
    return (margins, pair_loss)


def stats_kernel(local_ids, *refs, counts):
    n_in = len(counts)
    parts = refs[:n_in]
    *far, out, near, staged, rows, top, total, picked, arrived, landed = refs[n_in:]
    width = rows.shape[1]
    steps = near.shape[1] // BLOCK_ROWS

    def block(i):
        return pl.ds(pl.multiple_of(i * BLOCK_ROWS, BLOCK_ROWS), BLOCK_ROWS)

    def bringing(k, i):
        return pltpu.make_async_copy(far[k].at[block(i), :], near.at[k, block(i), :], arrived.at[k, i])

    begins = [ROWS * sum(counts[:n]) for n in range(n_in)]
    staging = [
        pltpu.make_async_copy(part, staged.at[pl.ds(begin, part.shape[0]), :], landed.at[n])
        for n, (part, begin) in enumerate(zip(parts, begins))
    ]
    for copy in staging:
        copy.start()
    for i in range(AHEAD):
        bringing(0, i).start()
        bringing(1, i).start()

    waited = 0
    for p in range(sum(counts) // 2):
        while waited < n_in and begins[waited] < (2 * p + 2) * ROWS:
            staging[waited].wait()
            waited += 1
        lanes = slice(p * 128, (p + 1) * 128)
        for x in range(4):
            at = 2 * p * ROWS + x * 448
            a, b = staged[at : at + 448, :], staged[at + ROWS : at + ROWS + 448, :]
            rows[2 * x * 448 : (2 * x + 1) * 448, lanes] = jnp.concatenate([a[:, :64], b[:, :64]], 1)
            rows[(2 * x + 1) * 448 : (2 * x + 2) * 448, lanes] = jnp.concatenate([a[:, 64:], b[:, 64:]], 1)
    top[...] = jnp.full_like(top, -jnp.inf)
    total[...] = jnp.zeros_like(total)
    picked[...] = jnp.zeros_like(picked)

    def step(i, carry):
        @pl.when(i + AHEAD < steps)
        def _():
            bringing(0, i + AHEAD).start()
            bringing(1, i + AHEAD).start()

        bringing(0, i).wait()
        bringing(1, i).wait()
        for k in range(2):
            logits = jnp.dot(near[k, block(i), :], rows[...], preferred_element_type=jnp.float32)
            tiles = logits.reshape(BLOCK_ROWS // 8, 8, width)
            before = top[...]
            now = jnp.maximum(before, jnp.max(tiles, 0))
            total[...] = total[...] * jnp.exp(before - now) + jnp.sum(jnp.exp(tiles - now[None]), 0)
            top[...] = now
            ids = lax.broadcasted_iota(jnp.int32, (BLOCK_ROWS, width), 0)
            hit = ids == local_ids[k : k + 1, :] - i * BLOCK_ROWS
            picked[...] += jnp.sum(jnp.where(hit, logits, 0.0).reshape(BLOCK_ROWS // 8, 8, width), 0)
        return carry

    lax.fori_loop(0, steps, step, 0)
    peak = jnp.max(top[...], 0, keepdims=True)
    mass = jnp.sum(total[...] * jnp.exp(top[...] - peak), 0, keepdims=True)
    out[0:1, :] = peak + jnp.log(mass)
    out[1:2, :] = jnp.sum(picked[...], 0, keepdims=True)


def chunk_stats(weights, local_ids, *parts):
    counts = tuple(part.shape[0] // ROWS for part in parts)
    width = 64 * sum(counts)
    vocab, depth = weights[0].shape
    near = pl.BlockSpec(memory_space=pltpu.VMEM)
    far = pl.BlockSpec(memory_space=pl.ANY)
    return pl.pallas_call(
        functools.partial(stats_kernel, counts=counts),
        in_specs=[near] + [far] * (len(parts) + 2),
        out_specs=near,
        out_shape=jax.ShapeDtypeStruct((2, width), jnp.float32),
        scratch_shapes=[
            pltpu.VMEM((2, vocab, depth), jnp.bfloat16),
            pltpu.VMEM((ROWS * sum(counts), 128), jnp.bfloat16),
            pltpu.VMEM((depth, width), jnp.bfloat16),
        ]
        + [pltpu.VMEM((8, width), jnp.float32)] * 3
        + [pltpu.SemaphoreType.DMA((2, vocab // BLOCK_ROWS)), pltpu.SemaphoreType.DMA((len(parts),))],
        compiler_params=pltpu.CompilerParams(vmem_limit_bytes=(width // 256 * 7 + 32) * 2**20),
        cost_estimate=pl.CostEstimate(
            flops=4 * width * vocab * depth, bytes_accessed=4 * vocab * depth, transcendentals=2 * vocab * width
        ),
    )(local_ids, *parts, *[pltpu.with_memory_space_constraint(w, pltpu.HBM) for w in weights])


def body(hidden, weight, targets, slot, prompt_len, ref_means):
    y, z, x, c = (lax.axis_index(axis) for axis in EVERY)
    vocab_cols = weight.shape[1]
    w_own = weight.T
    mine = hidden.T

    theirs = lax.ppermute(mine, C, SWAP)
    theirs, weight_sent = lax.optimization_barrier((theirs, w_own))
    w_other = lax.ppermute(weight_sent, C, SWAP)
    weights = [w_own, w_other]
    low = jnp.concatenate([mine[:, :64], theirs[:, :64]], 1)
    high = jnp.concatenate([theirs[:, 64:], mine[:, 64:]], 1)
    half = jnp.where(c == 0, low, high)
    behind, ahead, across = (lax.ppermute(half, X, ring_pairs(s)) for s in (1, 3, 2))
    turned = jnp.concatenate([half, ahead, across, behind, half, ahead, across], 0)
    own = lax.dynamic_slice_in_dim(turned, lax.rem(4 - x, 4) * 448, 1792, 0)

    off_y, off_z = jnp.where(c == 0, ALONG_B, ALONG_A), jnp.where(c == 0, ALONG_A, ALONG_B)
    source = (y + off_y) % 4 * 4 + (z + off_z) % 4
    ids = jnp.take(targets.reshape(32, 64), source * 2 + c, axis=0).reshape(1, 1024)
    start = lambda core: (((x * 2 + core) * 4 + y) * 4 + z) * vocab_cols
    local_ids = jnp.concatenate([ids - start(c), ids - start(1 - c)], 0)

    a_behind, a_ahead, *a_across = (shifted(own, True, k) for k in (1, 3, 2))
    upper = jnp.concatenate([own, a_behind], 0)
    lower = jnp.concatenate([a_ahead, *a_across], 0)
    behind_upper, ahead_lower = shifted(upper, False, 1), shifted(lower, False, 3)
    behind_lower, ahead_upper = shifted(lower, False, 1), shifted(upper, False, 3)
    first = chunk_stats(weights, local_ids[:, :256], upper, lower)
    behind_upper, ahead_lower, first = lax.optimization_barrier((behind_upper, ahead_lower, first))
    across = [shifted(behind_upper, False, 1), shifted(ahead_lower, False, 3)]
    second = chunk_stats(weights, local_ids[:, 256:512], behind_upper, ahead_lower)
    behind_lower, ahead_upper, across, second = lax.optimization_barrier((behind_lower, ahead_upper, across, second))
    third = chunk_stats(weights, local_ids[:, 512:], behind_lower, ahead_upper, *across)
    stats = jnp.concatenate([first, second, third], 1).reshape(2, 16, 64)
    group = np.arange(16, dtype=np.int32)
    ahead_y, ahead_z = (group // 4 - y) % 4, (group % 4 - z) % 4
    ahead = jnp.where(c == 0, ahead_z * 4 + ahead_y, ahead_y * 4 + ahead_z)
    at = jnp.sum(jnp.where(ahead[:, None] == np.arange(16)[None, :], PLACE[None, :], 0), axis=1)
    stats = jnp.take(stats, at, axis=1).reshape(2, 1024)

    copies = jnp.broadcast_to(stats, (64, 2, 1024))
    parts = lax.all_to_all(copies, CHIPS, split_axis=0, concat_axis=0, tiled=True)
    peak = jnp.max(parts[:, 0], 0)
    mass = jnp.sum(jnp.exp(parts[:, 0] - peak), 0)
    token_lp = (jnp.sum(parts[:, 1], 0) - (peak + jnp.log(mass))).reshape(16, 64)
    other_lp = lax.ppermute(token_lp, C, SWAP)
    per_seq = jnp.where(
        c == 0, jnp.concatenate([token_lp, other_lp], 1), jnp.concatenate([other_lp, token_lp], 1)
    )
    own_rows = lax.dynamic_slice_in_dim(per_seq, y * 4 + z, 1, 0).reshape(128)
    margins, pair_loss = finish(per_seq, slot, prompt_len, ref_means)
    return (own_rows, margins, pair_loss)


def solution(mesh):
    split = Mesh(mesh.devices.reshape(4, 4, 4, 2), EVERY)
    in_specs = (P(TOK, VOC), P(None, VOC_TOK), P(), P(), P(), P())
    out_specs = (P(TOK), P(), P())
    return jax.shard_map(body, mesh=split, in_specs=in_specs, out_specs=out_specs, check_vma=False)
```

```python
import functools

import jax
import jax.numpy as jnp
import numpy as np
from jax import lax
from jax.experimental import pallas as pl
from jax.experimental.pallas import tpu as pltpu
from jax.sharding import Mesh
from jax.sharding import PartitionSpec as P

Y, Z, X, C = "tok_0", "tok_1", "voc_0", "voc_1"
VOC = (X, C)
TOK = (Y, Z)
VOC_TOK = (X, C, Y, Z)
CHIPS = (Y, Z, X)
EVERY = (Y, Z, X, C)

RING = 4
SWAP = [(0, 1), (1, 0)]
ALONG_A = np.array([0, 3, 1, 2, 0, 3, 1, 2, 1, 2, 0, 3, 0, 3, 1, 2], np.int32)
ALONG_B = np.array([0, 0, 0, 0, 3, 3, 1, 1, 3, 3, 1, 1, 2, 2, 2, 2], np.int32)
PLACE = np.zeros(16, np.int32)
PLACE[ALONG_A * 4 + ALONG_B] = np.arange(16)
ROWS = 1792
BLOCK_ROWS = 400

beta_scale = 2.0


def ring_pairs(step):
    return [(i, (i + step) % RING) for i in range(RING)]


def crossed_pairs(first, step):
    pairs = []
    for y in range(4):
        for z in range(4):
            for x in range(4):
                for c in range(2):
                    along_z = (c == 0) == first
                    y2, z2 = (y, (z + step) % RING) if along_z else ((y + step) % RING, z)
                    pairs.append((((y * 4 + z) * 4 + x) * 2 + c, ((y2 * 4 + z2) * 4 + x) * 2 + c))
    return pairs


def shifted(block, first, step):
    return lax.ppermute(block, EVERY, crossed_pairs(first, step))


def finish(per_seq, slot, prompt_len, ref_means):
    seq_count, seq_width = per_seq.shape
    position = jnp.arange(seq_width, dtype=jnp.int32)[None, :]
    in_reply = position >= prompt_len[:, None]
    reply_len = (seq_width - prompt_len).astype(jnp.float32)
    seq_means = jnp.sum(jnp.where(in_reply, per_seq, jnp.float32(0.0)), axis=1) / reply_len
    advantage = seq_means - ref_means
    polarity = jnp.where(slot % 2 == 0, jnp.float32(1.0), jnp.float32(-1.0))
    n_pairs = seq_count // 2
    onehot = slot[:, None] // 2 == jnp.arange(n_pairs, dtype=jnp.int32)[None, :]
    signed = (polarity * advantage)[:, None]
    margins = beta_scale * jnp.sum(jnp.where(onehot, signed, jnp.float32(0.0)), axis=0)
    pair_loss = jnp.mean(jax.nn.softplus(-margins))
    return (margins, pair_loss)


def stats_kernel(local_ids, *refs, counts):
    n_in = len(counts)
    parts = refs[:n_in]
    *far, out, near, staged, rows, top, total, picked, arrived, landed = refs[n_in:]
    width = rows.shape[1]
    steps = near.shape[1] // BLOCK_ROWS

    def block(i):
        return pl.ds(pl.multiple_of(i * BLOCK_ROWS, BLOCK_ROWS), BLOCK_ROWS)

    def bringing(k, i):
        return pltpu.make_async_copy(far[k].at[block(i), :], near.at[k, block(i), :], arrived.at[k, i])

    begins = [ROWS * sum(counts[:n]) for n in range(n_in)]
    staging = [
        pltpu.make_async_copy(part, staged.at[pl.ds(begin, part.shape[0]), :], landed.at[n])
        for n, (part, begin) in enumerate(zip(parts, begins))
    ]
    for copy in staging:
        copy.start()
    bringing(0, 0).start()

    waited = 0
    for p in range(sum(counts) // 2):
        while waited < n_in and begins[waited] < (2 * p + 2) * ROWS:
            staging[waited].wait()
            waited += 1
        if p == 0:
            bringing(1, 0).start()
        lanes = slice(p * 128, (p + 1) * 128)
        for x in range(4):
            at = 2 * p * ROWS + x * 448
            a, b = staged[at : at + 448, :], staged[at + ROWS : at + ROWS + 448, :]
            rows[2 * x * 448 : (2 * x + 1) * 448, lanes] = jnp.concatenate([a[:, :64], b[:, :64]], 1)
            rows[(2 * x + 1) * 448 : (2 * x + 2) * 448, lanes] = jnp.concatenate([a[:, 64:], b[:, 64:]], 1)
    top[...] = jnp.full_like(top, -jnp.inf)
    total[...] = jnp.zeros_like(total)
    picked[...] = jnp.zeros_like(picked)

    def step(i, carry):
        @pl.when(i + 1 < steps)
        def _():
            bringing(0, i + 1).start()
            bringing(1, i + 1).start()

        bringing(0, i).wait()
        bringing(1, i).wait()
        for k in range(2):
            logits = jnp.dot(near[k, block(i), :], rows[...], preferred_element_type=jnp.float32)
            tiles = logits.reshape(BLOCK_ROWS // 8, 8, width)
            before = top[...]
            now = jnp.maximum(before, jnp.max(tiles, 0))
            total[...] = total[...] * jnp.exp(before - now) + jnp.sum(jnp.exp(tiles - now[None]), 0)
            top[...] = now
            ids = lax.broadcasted_iota(jnp.int32, (BLOCK_ROWS, width), 0)
            hit = ids == local_ids[k : k + 1, :] - i * BLOCK_ROWS
            picked[...] += jnp.sum(jnp.where(hit, logits, 0.0).reshape(BLOCK_ROWS // 8, 8, width), 0)
        return carry

    lax.fori_loop(0, steps, step, 0)
    peak = jnp.max(top[...], 0, keepdims=True)
    mass = jnp.sum(total[...] * jnp.exp(top[...] - peak), 0, keepdims=True)
    out[0:1, :] = peak + jnp.log(mass)
    out[1:2, :] = jnp.sum(picked[...], 0, keepdims=True)


def chunk_stats(weights, local_ids, *parts):
    counts = tuple(part.shape[0] // ROWS for part in parts)
    width = 64 * sum(counts)
    vocab, depth = weights[0].shape
    near = pl.BlockSpec(memory_space=pltpu.VMEM)
    far = pl.BlockSpec(memory_space=pl.ANY)
    return pl.pallas_call(
        functools.partial(stats_kernel, counts=counts),
        in_specs=[near] + [far] * (len(parts) + 2),
        out_specs=near,
        out_shape=jax.ShapeDtypeStruct((2, width), jnp.float32),
        scratch_shapes=[
            pltpu.VMEM((2, vocab, depth), jnp.bfloat16),
            pltpu.VMEM((ROWS * sum(counts), 128), jnp.bfloat16),
            pltpu.VMEM((depth, width), jnp.bfloat16),
        ]
        + [pltpu.VMEM((8, width), jnp.float32)] * 3
        + [pltpu.SemaphoreType.DMA((2, vocab // BLOCK_ROWS)), pltpu.SemaphoreType.DMA((len(parts),))],
        compiler_params=pltpu.CompilerParams(vmem_limit_bytes=(width // 256 * 7 + 32) * 2**20),
        cost_estimate=pl.CostEstimate(
            flops=4 * width * vocab * depth, bytes_accessed=4 * vocab * depth, transcendentals=2 * vocab * width
        ),
    )(local_ids, *parts, *[pltpu.with_memory_space_constraint(w, pltpu.HBM) for w in weights])


def body(hidden, weight, targets, slot, prompt_len, ref_means):
    y, z, x, c = (lax.axis_index(axis) for axis in EVERY)
    vocab_cols = weight.shape[1]
    w_own = weight.T
    mine = hidden.T

    theirs = lax.ppermute(mine, C, SWAP)
    theirs, weight_sent = lax.optimization_barrier((theirs, w_own))
    w_other = lax.ppermute(weight_sent, C, SWAP)
    weights = [w_own, w_other]
    low = jnp.concatenate([mine[:, :64], theirs[:, :64]], 1)
    high = jnp.concatenate([theirs[:, 64:], mine[:, 64:]], 1)
    half = jnp.where(c == 0, low, high)
    behind, ahead, across = (lax.ppermute(half, X, ring_pairs(s)) for s in (1, 3, 2))
    turned = jnp.concatenate([half, ahead, across, behind, half, ahead, across], 0)
    own = lax.dynamic_slice_in_dim(turned, lax.rem(4 - x, 4) * 448, 1792, 0)

    a_behind, a_ahead, *a_across = (shifted(own, True, k) for k in (1, 3, 2))
    a_behind, targets, y, z, c = lax.optimization_barrier((a_behind, targets, y, z, c))

    off_y, off_z = jnp.where(c == 0, ALONG_B, ALONG_A), jnp.where(c == 0, ALONG_A, ALONG_B)
    source = (y + off_y) % 4 * 4 + (z + off_z) % 4
    ids = jnp.take(targets.reshape(32, 64), source * 2 + c, axis=0).reshape(1, 1024)
    start = lambda core: (((x * 2 + core) * 4 + y) * 4 + z) * vocab_cols
    local_ids = jnp.concatenate([ids - start(c), ids - start(1 - c)], 0)
    group = np.arange(16, dtype=np.int32)
    ahead_y, ahead_z = (group // 4 - y) % 4, (group % 4 - z) % 4
    ahead = jnp.where(c == 0, ahead_z * 4 + ahead_y, ahead_y * 4 + ahead_z)
    at = jnp.sum(jnp.where(ahead[:, None] == np.arange(16)[None, :], PLACE[None, :], 0), axis=1)
    a_ahead, a_across, local_ids, at = lax.optimization_barrier((a_ahead, a_across, local_ids, at))

    upper = jnp.concatenate([own, a_behind], 0)
    lower = jnp.concatenate([a_ahead, *a_across], 0)
    behind_upper, ahead_lower = shifted(upper, False, 1), shifted(lower, False, 3)
    behind_lower, ahead_upper = shifted(lower, False, 1), shifted(upper, False, 3)
    first = chunk_stats(weights, local_ids[:, :256], upper, lower)
    behind_upper, ahead_lower, first = lax.optimization_barrier((behind_upper, ahead_lower, first))
    across = [shifted(behind_upper, False, 1), shifted(ahead_lower, False, 3)]
    second = chunk_stats(weights, local_ids[:, 256:512], behind_upper, ahead_lower)
    behind_lower, ahead_upper, across, second = lax.optimization_barrier((behind_lower, ahead_upper, across, second))
    third = chunk_stats(weights, local_ids[:, 512:], behind_lower, ahead_upper, *across)
    stats = jnp.concatenate([first, second, third], 1).reshape(2, 16, 64)
    stats = jnp.take(stats, at, axis=1).reshape(2, 1024)

    copies = jnp.broadcast_to(stats, (64, 2, 1024))
    parts = lax.all_to_all(copies, CHIPS, split_axis=0, concat_axis=0, tiled=True)
    peak = jnp.max(parts[:, 0], 0)
    mass = jnp.sum(jnp.exp(parts[:, 0] - peak), 0)
    token_lp = (jnp.sum(parts[:, 1], 0) - (peak + jnp.log(mass))).reshape(16, 64)
    other_lp = lax.ppermute(token_lp, C, SWAP)
    per_seq = jnp.where(
        c == 0, jnp.concatenate([token_lp, other_lp], 1), jnp.concatenate([other_lp, token_lp], 1)
    )
    own_rows = lax.dynamic_slice_in_dim(per_seq, y * 4 + z, 1, 0).reshape(128)
    margins, pair_loss = finish(per_seq, slot, prompt_len, ref_means)
    return (own_rows, margins, pair_loss)


def solution(mesh):
    split = Mesh(mesh.devices.reshape(4, 4, 4, 2), EVERY)
    in_specs = (P(TOK, VOC), P(None, VOC_TOK), P(), P(), P(), P())
    out_specs = (P(TOK), P(), P())
    return jax.shard_map(body, mesh=split, in_specs=in_specs, out_specs=out_specs, check_vma=False)
```

```python
import functools

import jax
import jax.numpy as jnp
import numpy as np
from jax import lax
from jax.experimental import pallas as pl
from jax.experimental.pallas import tpu as pltpu
from jax.sharding import Mesh
from jax.sharding import PartitionSpec as P

Y, Z, X, C = "tok_0", "tok_1", "voc_0", "voc_1"
VOC = (X, C)
TOK = (Y, Z)
VOC_TOK = (X, C, Y, Z)
CHIPS = (Y, Z, X)
EVERY = (Y, Z, X, C)

RING = 4
SWAP = [(0, 1), (1, 0)]
ALONG_A = np.array([0, 3, 1, 2, 0, 3, 1, 2, 1, 2, 0, 3, 0, 3, 1, 2], np.int32)
ALONG_B = np.array([0, 0, 0, 0, 3, 3, 1, 1, 3, 3, 1, 1, 2, 2, 2, 2], np.int32)
PLACE = np.zeros(16, np.int32)
PLACE[ALONG_A * 4 + ALONG_B] = np.arange(16)
ROWS = 1792
BLOCK_ROWS = 400

beta_scale = 2.0


def ring_pairs(step):
    return [(i, (i + step) % RING) for i in range(RING)]


def crossed_pairs(first, step):
    pairs = []
    for y in range(4):
        for z in range(4):
            for x in range(4):
                for c in range(2):
                    along_z = (c == 0) == first
                    y2, z2 = (y, (z + step) % RING) if along_z else ((y + step) % RING, z)
                    pairs.append((((y * 4 + z) * 4 + x) * 2 + c, ((y2 * 4 + z2) * 4 + x) * 2 + c))
    return pairs


def shifted(block, first, step):
    return lax.ppermute(block, EVERY, crossed_pairs(first, step))


def finish(per_seq, slot, prompt_len, ref_means):
    seq_count, seq_width = per_seq.shape
    position = jnp.arange(seq_width, dtype=jnp.int32)[None, :]
    in_reply = position >= prompt_len[:, None]
    reply_len = (seq_width - prompt_len).astype(jnp.float32)
    seq_means = jnp.sum(jnp.where(in_reply, per_seq, jnp.float32(0.0)), axis=1) / reply_len
    advantage = seq_means - ref_means
    polarity = jnp.where(slot % 2 == 0, jnp.float32(1.0), jnp.float32(-1.0))
    n_pairs = seq_count // 2
    onehot = slot[:, None] // 2 == jnp.arange(n_pairs, dtype=jnp.int32)[None, :]
    signed = (polarity * advantage)[:, None]
    margins = beta_scale * jnp.sum(jnp.where(onehot, signed, jnp.float32(0.0)), axis=0)
    pair_loss = jnp.mean(jax.nn.softplus(-margins))
    return (margins, pair_loss)


def stats_kernel(local_ids, *refs, counts):
    n_in = len(counts)
    parts = refs[:n_in]
    *far, out, near, staged, rows, top, total, picked, arrived, landed = refs[n_in:]
    width = rows.shape[1]
    steps = near.shape[1] // BLOCK_ROWS

    def block(i):
        return pl.ds(pl.multiple_of(i * BLOCK_ROWS, BLOCK_ROWS), BLOCK_ROWS)

    def bringing(k, i):
        return pltpu.make_async_copy(far[k].at[block(i), :], near.at[k, block(i), :], arrived.at[k, i])

    begins = [ROWS * sum(counts[:n]) for n in range(n_in)]
    staging = [
        pltpu.make_async_copy(part, staged.at[pl.ds(begin, part.shape[0]), :], landed.at[n])
        for n, (part, begin) in enumerate(zip(parts, begins))
    ]
    for copy in staging:
        copy.start()
    ahead = 2 if width <= 256 else 1
    bringing(0, 0).start()
    for i in range(1, ahead):
        bringing(1, i - 1).start()
        bringing(0, i).start()

    waited = 0
    for p in range(sum(counts) // 2):
        while waited < n_in and begins[waited] < (2 * p + 2) * ROWS:
            staging[waited].wait()
            waited += 1
        if p == 0:
            bringing(1, ahead - 1).start()
        lanes = slice(p * 128, (p + 1) * 128)
        for x in range(4):
            at = 2 * p * ROWS + x * 448
            a, b = staged[at : at + 448, :], staged[at + ROWS : at + ROWS + 448, :]
            rows[2 * x * 448 : (2 * x + 1) * 448, lanes] = jnp.concatenate([a[:, :64], b[:, :64]], 1)
            rows[(2 * x + 1) * 448 : (2 * x + 2) * 448, lanes] = jnp.concatenate([a[:, 64:], b[:, 64:]], 1)
    top[...] = jnp.full_like(top, -jnp.inf)
    total[...] = jnp.zeros_like(total)
    picked[...] = jnp.zeros_like(picked)

    def step(i, carry):
        @pl.when(i + ahead < steps)
        def _():
            bringing(0, i + ahead).start()
            bringing(1, i + ahead).start()

        bringing(0, i).wait()
        bringing(1, i).wait()
        for k in range(2):
            logits = jnp.dot(near[k, block(i), :], rows[...], preferred_element_type=jnp.float32)
            tiles = logits.reshape(BLOCK_ROWS // 8, 8, width)
            before = top[...]
            now = jnp.maximum(before, jnp.max(tiles, 0))
            total[...] = total[...] * jnp.exp(before - now) + jnp.sum(jnp.exp(tiles - now[None]), 0)
            top[...] = now
            ids = lax.broadcasted_iota(jnp.int32, (BLOCK_ROWS, width), 0)
            hit = ids == local_ids[k : k + 1, :] - i * BLOCK_ROWS
            picked[...] += jnp.sum(jnp.where(hit, logits, 0.0).reshape(BLOCK_ROWS // 8, 8, width), 0)
        return carry

    lax.fori_loop(0, steps, step, 0)
    peak = jnp.max(top[...], 0, keepdims=True)
    mass = jnp.sum(total[...] * jnp.exp(top[...] - peak), 0, keepdims=True)
    out[0:1, :] = peak + jnp.log(mass)
    out[1:2, :] = jnp.sum(picked[...], 0, keepdims=True)


def chunk_stats(weights, local_ids, *parts):
    counts = tuple(part.shape[0] // ROWS for part in parts)
    width = 64 * sum(counts)
    vocab, depth = weights[0].shape
    near = pl.BlockSpec(memory_space=pltpu.VMEM)
    far = pl.BlockSpec(memory_space=pl.ANY)
    return pl.pallas_call(
        functools.partial(stats_kernel, counts=counts),
        in_specs=[near] + [far] * (len(parts) + 2),
        out_specs=near,
        out_shape=jax.ShapeDtypeStruct((2, width), jnp.float32),
        scratch_shapes=[
            pltpu.VMEM((2, vocab, depth), jnp.bfloat16),
            pltpu.VMEM((ROWS * sum(counts), 128), jnp.bfloat16),
            pltpu.VMEM((depth, width), jnp.bfloat16),
        ]
        + [pltpu.VMEM((8, width), jnp.float32)] * 3
        + [pltpu.SemaphoreType.DMA((2, vocab // BLOCK_ROWS)), pltpu.SemaphoreType.DMA((len(parts),))],
        compiler_params=pltpu.CompilerParams(vmem_limit_bytes=(width // 256 * 7 + 32) * 2**20),
        cost_estimate=pl.CostEstimate(
            flops=4 * width * vocab * depth, bytes_accessed=4 * vocab * depth, transcendentals=2 * vocab * width
        ),
    )(local_ids, *parts, *[pltpu.with_memory_space_constraint(w, pltpu.HBM) for w in weights])


def body(hidden, weight, targets, slot, prompt_len, ref_means):
    y, z, x, c = (lax.axis_index(axis) for axis in EVERY)
    vocab_cols = weight.shape[1]
    w_own = weight.T
    mine = hidden.T

    theirs = lax.ppermute(mine, C, SWAP)
    theirs, weight_sent = lax.optimization_barrier((theirs, w_own))
    w_other = lax.ppermute(weight_sent, C, SWAP)
    weights = [w_own, w_other]
    low = jnp.concatenate([mine[:, :64], theirs[:, :64]], 1)
    high = jnp.concatenate([theirs[:, 64:], mine[:, 64:]], 1)
    half = jnp.where(c == 0, low, high)
    behind, ahead, across = (lax.ppermute(half, X, ring_pairs(s)) for s in (1, 3, 2))
    turned = jnp.concatenate([half, ahead, across, behind, half, ahead, across], 0)
    own = lax.dynamic_slice_in_dim(turned, lax.rem(4 - x, 4) * 448, 1792, 0)

    a_behind, a_ahead, *a_across = (shifted(own, True, k) for k in (1, 3, 2))
    a_behind, targets, y, z, c = lax.optimization_barrier((a_behind, targets, y, z, c))

    off_y, off_z = jnp.where(c == 0, ALONG_B, ALONG_A), jnp.where(c == 0, ALONG_A, ALONG_B)
    source = (y + off_y) % 4 * 4 + (z + off_z) % 4
    ids = jnp.take(targets.reshape(32, 64), source * 2 + c, axis=0).reshape(1, 1024)
    start = lambda core: (((x * 2 + core) * 4 + y) * 4 + z) * vocab_cols
    local_ids = jnp.concatenate([ids - start(c), ids - start(1 - c)], 0)
    group = np.arange(16, dtype=np.int32)
    ahead_y, ahead_z = (group // 4 - y) % 4, (group % 4 - z) % 4
    ahead = jnp.where(c == 0, ahead_z * 4 + ahead_y, ahead_y * 4 + ahead_z)
    at = jnp.sum(jnp.where(ahead[:, None] == np.arange(16)[None, :], PLACE[None, :], 0), axis=1)
    a_ahead, a_across, local_ids, at = lax.optimization_barrier((a_ahead, a_across, local_ids, at))

    upper = jnp.concatenate([own, a_behind], 0)
    lower = jnp.concatenate([a_ahead, *a_across], 0)
    behind_upper, ahead_lower = shifted(upper, False, 1), shifted(lower, False, 3)
    upper_later, lower = lax.optimization_barrier((upper, lower))
    behind_lower, ahead_upper = shifted(lower, False, 1), shifted(upper_later, False, 3)
    first = chunk_stats(weights, local_ids[:, :256], upper, lower)
    behind_upper, ahead_lower, first = lax.optimization_barrier((behind_upper, ahead_lower, first))
    across = [shifted(behind_upper, False, 1), shifted(ahead_lower, False, 3)]
    second = chunk_stats(weights, local_ids[:, 256:512], behind_upper, ahead_lower)
    behind_lower, ahead_upper, across, second = lax.optimization_barrier((behind_lower, ahead_upper, across, second))
    third = chunk_stats(weights, local_ids[:, 512:], behind_lower, ahead_upper, *across)
    stats = jnp.concatenate([first, second, third], 1).reshape(2, 16, 64)
    stats = jnp.take(stats, at, axis=1).reshape(2, 1024)

    copies = jnp.broadcast_to(stats, (64, 2, 1024))
    parts = lax.all_to_all(copies, CHIPS, split_axis=0, concat_axis=0, tiled=True)
    peak = jnp.max(parts[:, 0], 0)
    mass = jnp.sum(jnp.exp(parts[:, 0] - peak), 0)
    token_lp = (jnp.sum(parts[:, 1], 0) - (peak + jnp.log(mass))).reshape(16, 64)
    other_lp = lax.ppermute(token_lp, C, SWAP)
    per_seq = jnp.where(
        c == 0, jnp.concatenate([token_lp, other_lp], 1), jnp.concatenate([other_lp, token_lp], 1)
    )
    own_rows = lax.dynamic_slice_in_dim(per_seq, y * 4 + z, 1, 0).reshape(128)
    margins, pair_loss = finish(per_seq, slot, prompt_len, ref_means)
    return (own_rows, margins, pair_loss)


def solution(mesh):
    split = Mesh(mesh.devices.reshape(4, 4, 4, 2), EVERY)
    in_specs = (P(TOK, VOC), P(None, VOC_TOK), P(), P(), P(), P())
    out_specs = (P(TOK), P(), P())
    return jax.shard_map(body, mesh=split, in_specs=in_specs, out_specs=out_specs, check_vma=False)
```

```python
import functools

import jax
import jax.numpy as jnp
import numpy as np
from jax import lax
from jax.experimental import pallas as pl
from jax.experimental.pallas import tpu as pltpu
from jax.sharding import Mesh
from jax.sharding import PartitionSpec as P

Y, Z, X, C = "tok_0", "tok_1", "voc_0", "voc_1"
VOC = (X, C)
TOK = (Y, Z)
VOC_TOK = (X, C, Y, Z)
CHIPS = (Y, Z, X)
EVERY = (Y, Z, X, C)

RING = 4
SWAP = [(0, 1), (1, 0)]
ALONG_A = np.array([0, 3, 1, 2, 0, 3, 1, 2, 1, 2, 0, 3, 0, 3, 1, 2], np.int32)
ALONG_B = np.array([0, 0, 0, 0, 3, 3, 1, 1, 3, 3, 1, 1, 2, 2, 2, 2], np.int32)
PLACE = np.zeros(16, np.int32)
PLACE[ALONG_A * 4 + ALONG_B] = np.arange(16)
ROWS = 1792
BLOCK_ROWS = 400

beta_scale = 2.0


def ring_pairs(step):
    return [(i, (i + step) % RING) for i in range(RING)]


def crossed_pairs(first, step):
    pairs = []
    for y in range(4):
        for z in range(4):
            for x in range(4):
                for c in range(2):
                    along_z = (c == 0) == first
                    y2, z2 = (y, (z + step) % RING) if along_z else ((y + step) % RING, z)
                    pairs.append((((y * 4 + z) * 4 + x) * 2 + c, ((y2 * 4 + z2) * 4 + x) * 2 + c))
    return pairs


def shifted(block, first, step):
    return lax.ppermute(block, EVERY, crossed_pairs(first, step))


def finish(per_seq, slot, prompt_len, ref_means):
    seq_count, seq_width = per_seq.shape
    position = jnp.arange(seq_width, dtype=jnp.int32)[None, :]
    in_reply = position >= prompt_len[:, None]
    reply_len = (seq_width - prompt_len).astype(jnp.float32)
    seq_means = jnp.sum(jnp.where(in_reply, per_seq, jnp.float32(0.0)), axis=1) / reply_len
    advantage = seq_means - ref_means
    polarity = jnp.where(slot % 2 == 0, jnp.float32(1.0), jnp.float32(-1.0))
    n_pairs = seq_count // 2
    onehot = slot[:, None] // 2 == jnp.arange(n_pairs, dtype=jnp.int32)[None, :]
    signed = (polarity * advantage)[:, None]
    margins = beta_scale * jnp.sum(jnp.where(onehot, signed, jnp.float32(0.0)), axis=0)
    pair_loss = jnp.mean(jax.nn.softplus(-margins))
    return (margins, pair_loss)


def stats_kernel(local_ids, *refs, counts):
    n_in = len(counts)
    parts = refs[:n_in]
    *far, out, near, staged, rows, top, total, picked, arrived, landed = refs[n_in:]
    width = rows.shape[1]
    steps = near.shape[1] // BLOCK_ROWS

    def block(i):
        return pl.ds(pl.multiple_of(i * BLOCK_ROWS, BLOCK_ROWS), BLOCK_ROWS)

    def bringing(k, i):
        return pltpu.make_async_copy(far[k].at[block(i), :], near.at[k, block(i), :], arrived.at[k, i])

    begins = [ROWS * sum(counts[:n]) for n in range(n_in)]
    staging = [
        pltpu.make_async_copy(part, staged.at[pl.ds(begin, part.shape[0]), :], landed.at[n])
        for n, (part, begin) in enumerate(zip(parts, begins))
    ]
    for copy in staging:
        copy.start()
    ahead = 2 if width <= 256 else 1
    bringing(0, 0).start()
    for i in range(1, ahead):
        bringing(1, i - 1).start()
        bringing(0, i).start()

    waited = 0
    for p in range(sum(counts) // 2):
        while waited < n_in and begins[waited] < (2 * p + 2) * ROWS:
            staging[waited].wait()
            waited += 1
        if p == 0:
            bringing(1, ahead - 1).start()
        lanes = slice(p * 128, (p + 1) * 128)
        for x in range(4):
            at = 2 * p * ROWS + x * 448
            a, b = staged[at : at + 448, :], staged[at + ROWS : at + ROWS + 448, :]
            rows[2 * x * 448 : (2 * x + 1) * 448, lanes] = jnp.concatenate([a[:, :64], b[:, :64]], 1)
            rows[(2 * x + 1) * 448 : (2 * x + 2) * 448, lanes] = jnp.concatenate([a[:, 64:], b[:, 64:]], 1)
    top[...] = jnp.full_like(top, -jnp.inf)
    total[...] = jnp.zeros_like(total)
    picked[...] = jnp.zeros_like(picked)

    def step(i, carry):
        @pl.when(i + ahead < steps)
        def _():
            bringing(0, i + ahead).start()
            bringing(1, i + ahead).start()

        bringing(0, i).wait()
        bringing(1, i).wait()
        for k in range(2):
            logits = jnp.dot(near[k, block(i), :], rows[...], preferred_element_type=jnp.float32)
            tiles = logits.reshape(BLOCK_ROWS // 8, 8, width)
            before = top[...]
            now = jnp.maximum(before, jnp.max(tiles, 0))
            total[...] = total[...] * jnp.exp(before - now) + jnp.sum(jnp.exp(tiles - now[None]), 0)
            top[...] = now
            ids = lax.broadcasted_iota(jnp.int32, (BLOCK_ROWS, width), 0)
            hit = ids == local_ids[k : k + 1, :] - i * BLOCK_ROWS
            picked[...] += jnp.sum(jnp.where(hit, logits, 0.0).reshape(BLOCK_ROWS // 8, 8, width), 0)
        return carry

    lax.fori_loop(0, steps, step, 0)
    peak = jnp.max(top[...], 0, keepdims=True)
    mass = jnp.sum(total[...] * jnp.exp(top[...] - peak), 0, keepdims=True)
    out[0:1, :] = peak + jnp.log(mass)
    out[1:2, :] = jnp.sum(picked[...], 0, keepdims=True)


def chunk_stats(weights, local_ids, *parts):
    counts = tuple(part.shape[0] // ROWS for part in parts)
    width = 64 * sum(counts)
    vocab, depth = weights[0].shape
    near = pl.BlockSpec(memory_space=pltpu.VMEM)
    far = pl.BlockSpec(memory_space=pl.ANY)
    return pl.pallas_call(
        functools.partial(stats_kernel, counts=counts),
        in_specs=[near] + [far] * (len(parts) + 2),
        out_specs=near,
        out_shape=jax.ShapeDtypeStruct((2, width), jnp.float32),
        scratch_shapes=[
            pltpu.VMEM((2, vocab, depth), jnp.bfloat16),
            pltpu.VMEM((ROWS * sum(counts), 128), jnp.bfloat16),
            pltpu.VMEM((depth, width), jnp.bfloat16),
        ]
        + [pltpu.VMEM((8, width), jnp.float32)] * 3
        + [pltpu.SemaphoreType.DMA((2, vocab // BLOCK_ROWS)), pltpu.SemaphoreType.DMA((len(parts),))],
        compiler_params=pltpu.CompilerParams(vmem_limit_bytes=(width // 256 * 7 + 32) * 2**20),
        cost_estimate=pl.CostEstimate(
            flops=4 * width * vocab * depth, bytes_accessed=4 * vocab * depth, transcendentals=2 * vocab * width
        ),
    )(local_ids, *parts, *[pltpu.with_memory_space_constraint(w, pltpu.HBM) for w in weights])


def body(hidden, weight, targets, slot, prompt_len, ref_means):
    y, z, x, c = (lax.axis_index(axis) for axis in EVERY)
    vocab_cols = weight.shape[1]
    w_own = weight.T
    mine = hidden.T

    theirs = lax.ppermute(mine, C, SWAP)
    theirs, weight_sent = lax.optimization_barrier((theirs, w_own))
    w_other = lax.ppermute(weight_sent, C, SWAP)
    weights = [w_own, w_other]
    low = jnp.concatenate([mine[:, :64], theirs[:, :64]], 1)
    high = jnp.concatenate([theirs[:, 64:], mine[:, 64:]], 1)
    half = jnp.where(c == 0, low, high)
    behind, ahead, across = (lax.ppermute(half, X, ring_pairs(s)) for s in (1, 3, 2))
    turned = jnp.concatenate([half, ahead, across, behind, half, ahead, across], 0)
    own = lax.dynamic_slice_in_dim(turned, lax.rem(4 - x, 4) * 448, 1792, 0)

    a_behind, a_ahead, *a_across = (shifted(own, True, k) for k in (1, 3, 2))
    upper = jnp.concatenate([own, a_behind], 0)
    upper, targets, y, z, c = lax.optimization_barrier((upper, targets, y, z, c))

    off_y, off_z = jnp.where(c == 0, ALONG_B, ALONG_A), jnp.where(c == 0, ALONG_A, ALONG_B)
    source = (y + off_y) % 4 * 4 + (z + off_z) % 4
    ids = jnp.take(targets.reshape(32, 64), source * 2 + c, axis=0).reshape(1, 1024)
    start = lambda core: (((x * 2 + core) * 4 + y) * 4 + z) * vocab_cols
    local_ids = jnp.concatenate([ids - start(c), ids - start(1 - c)], 0)
    group = np.arange(16, dtype=np.int32)
    ahead_y, ahead_z = (group // 4 - y) % 4, (group % 4 - z) % 4
    ahead = jnp.where(c == 0, ahead_z * 4 + ahead_y, ahead_y * 4 + ahead_z)
    at = jnp.sum(jnp.where(ahead[:, None] == np.arange(16)[None, :], PLACE[None, :], 0), axis=1)
    a_ahead, a_across, local_ids, at = lax.optimization_barrier((a_ahead, a_across, local_ids, at))

    lower = jnp.concatenate([a_ahead, *a_across], 0)
    behind_upper, ahead_lower = shifted(upper, False, 1), shifted(lower, False, 3)
    upper_later, lower = lax.optimization_barrier((upper, lower))
    behind_lower, ahead_upper = shifted(lower, False, 1), shifted(upper_later, False, 3)
    first = chunk_stats(weights, local_ids[:, :256], upper, lower)
    behind_upper, ahead_lower, first = lax.optimization_barrier((behind_upper, ahead_lower, first))
    across = [shifted(behind_upper, False, 1), shifted(ahead_lower, False, 3)]
    second = chunk_stats(weights, local_ids[:, 256:512], behind_upper, ahead_lower)
    behind_lower, ahead_upper, across, second = lax.optimization_barrier((behind_lower, ahead_upper, across, second))
    third = chunk_stats(weights, local_ids[:, 512:], behind_lower, ahead_upper, *across)
    stats = jnp.concatenate([first, second, third], 1).reshape(2, 16, 64)
    stats = jnp.take(stats, at, axis=1).reshape(2, 1024)

    copies = jnp.broadcast_to(stats, (64, 2, 1024))
    parts = lax.all_to_all(copies, CHIPS, split_axis=0, concat_axis=0, tiled=True)
    peak = jnp.max(parts[:, 0], 0)
    mass = jnp.sum(jnp.exp(parts[:, 0] - peak), 0)
    token_lp = (jnp.sum(parts[:, 1], 0) - (peak + jnp.log(mass))).reshape(16, 64)
    other_lp = lax.ppermute(token_lp, C, SWAP)
    per_seq = jnp.where(
        c == 0, jnp.concatenate([token_lp, other_lp], 1), jnp.concatenate([other_lp, token_lp], 1)
    )
    own_rows = lax.dynamic_slice_in_dim(per_seq, y * 4 + z, 1, 0).reshape(128)
    margins, pair_loss = finish(per_seq, slot, prompt_len, ref_means)
    return (own_rows, margins, pair_loss)


def solution(mesh):
    split = Mesh(mesh.devices.reshape(4, 4, 4, 2), EVERY)
    in_specs = (P(TOK, VOC), P(None, VOC_TOK), P(), P(), P(), P())
    out_specs = (P(TOK), P(), P())
    return jax.shard_map(body, mesh=split, in_specs=in_specs, out_specs=out_specs, check_vma=False)
```
